128 devices in a mesh: dp: 8 (over x_lo, z), tensor: 16 (over x_hi, y, core).
Axes of the slice: x: 4 (x_hi: 2, x_lo: 2; x = x_hi * 2 + x_lo), y: 4, z: 4, core: 2. Of those that a mesh axis runs over, the one named last changes fastest.
Arguments:
- layer_input: bfloat16 [1024, 5376], P('tensor', 'dp'), may hold values from -6 to 6
- gate_weight: bfloat16 [5376, 21504], P('dp', 'tensor'), may hold values from -0.078125 to 0.078125
- up_weight: bfloat16 [5376, 21504], P('dp', 'tensor'), may hold values from -0.078125 to 0.078125
- down_weight: bfloat16 [21504, 5376], P('tensor', 'dp'), may hold values from -0.0390625 to 0.0390625
- granularity: int32 [16], replicated, may hold values from 0 to 3, as said below
- out_grad: bfloat16 [1024, 5376], P('tensor', 'dp'), may hold values from -4 to 4
Outputs:
- layer_output: bfloat16 [1024, 5376], P('tensor', 'dp')
- input_grad: bfloat16 [1024, 5376], P('tensor', 'dp')
- gate_grad: bfloat16 [5376, 21504], P('dp', 'tensor')
- up_grad: bfloat16 [5376, 21504], P('dp', 'tensor')
- down_grad: bfloat16 [21504, 5376], P('tensor', 'dp')
The draws below stay inside these ranges and needn't reach their ends.
Inputs may be any that keep to these rules, and one draw needn't show every extreme that they name: `granularity`: the nested level of each sequence; in every draw some sequence has level 0 and some has level 3.
All inputs are finite; a program needn't handle non-finite values.
Results may differ from the reference program's by a relative error of at most 0.0051.
Values may be sent and summed in bfloat16 or wider, within the bound.
A program may use at most 128 MiB of HBM per device.

```python
import jax
import jax.numpy as jnp
from jax import lax

D = 5376
FF = 21504
LEN = 64
SEQS = 16
TOKENS = 1024


def draw_granularity(key, part):
    key = jax.random.fold_in(key, 17)
    first_key, second_key = jax.random.split(key)
    levels = jax.random.randint(first_key, (SEQS,), 0, 4, dtype=jnp.int32)
    order = jax.random.permutation(second_key, SEQS)
    levels = levels.at[order[0]].set(3).at[order[1]].set(0)
    return levels.astype(jnp.int32)


def block_levels(stream_key, shape, pieces, smallest, high):
    loudness, own = 1.0, jax.random.fold_in(stream_key, 6)
    for dim, parts in pieces:
        steps = jnp.exp(jax.random.uniform(jax.random.fold_in(own, dim), (parts,), jnp.float32, smallest / len(pieces), high / len(pieces)))
        loudness = loudness * jnp.repeat(steps, shape[dim] // parts).reshape([-1 if axis == dim else 1 for axis in range(len(shape))])
    return loudness


def scatter_about(key, extent, deviation, reach, cuts=(), held_as=jnp.bfloat16):
    result = deviation * jax.random.normal(key, extent, jnp.float32)
    if cuts:
        result = result * block_levels(key, extent, cuts, -0.22, 0.18)
    return jnp.clip(result, -reach, reach).astype(held_as)


def setup_inputs(seed: int = 0) -> dict:
    streams_of = jax.random.split(jax.random.key(seed), 7)
    layer_input = scatter_about(streams_of[0], (TOKENS, D), 1.0, 6.0, ((0, 16), (1, 8)))
    gate_weight = scatter_about(streams_of[1], (D, FF), D ** -0.5, 0.078125, ((0, 8), (1, 16)))
    up_weight = scatter_about(streams_of[2], (D, FF), D ** -0.5, 0.078125, ((0, 8), (1, 16)))
    down_weight = scatter_about(streams_of[3], (FF, D), FF ** -0.5, 0.0390625, ((0, 16), (1, 8)))
    granularity = draw_granularity(jax.random.fold_in(streams_of[6], 71), 0)
    out_grad = scatter_about(streams_of[5], (TOKENS, D), 0.5, 4.0, ((0, 16), (1, 8)))
    return dict(layer_input=layer_input, gate_weight=gate_weight, up_weight=up_weight, down_weight=down_weight, granularity=granularity, out_grad=out_grad)


def contract(left, right, left_dim, right_dim):
    return lax.dot_general(left, right, (((left_dim,), (right_dim,)), ((), ())), preferred_element_type=jnp.float32)


def reference(layer_input, gate_weight, up_weight, down_weight, granularity, out_grad):
    widths = jnp.left_shift(jnp.int32(FF // 8), granularity.astype(jnp.int32))
    row_width = jnp.repeat(widths, LEN)
    col_index = jnp.arange(FF, dtype=jnp.int32)
    col_mask = (col_index[None, :] < row_width[:, None]).astype(jnp.float32)
    gate_pre = jnp.dot(layer_input, gate_weight, preferred_element_type=jnp.float32)
    up_pre = jnp.dot(layer_input, up_weight, preferred_element_type=jnp.float32)
    gate_sig = jax.nn.sigmoid(gate_pre)
    gate_act = gate_pre * gate_sig
    hidden = (gate_act * up_pre * col_mask).astype(jnp.bfloat16)
    layer_output = jnp.dot(hidden, down_weight, preferred_element_type=jnp.float32).astype(jnp.bfloat16)
    hidden_grad = contract(out_grad, down_weight, 1, 1)
    gate_delta = (hidden_grad * up_pre * gate_sig * (1.0 + gate_pre * (1.0 - gate_sig)) * col_mask).astype(jnp.bfloat16)
    up_delta = (hidden_grad * gate_act * col_mask).astype(jnp.bfloat16)
    down_grad = contract(hidden, out_grad, 0, 0).astype(jnp.bfloat16)
    gate_grad = contract(layer_input, gate_delta, 0, 0).astype(jnp.bfloat16)
    up_grad = contract(layer_input, up_delta, 0, 0).astype(jnp.bfloat16)
    input_grad = (contract(gate_delta, gate_weight, 1, 1) + contract(up_delta, up_weight, 1, 1)).astype(jnp.bfloat16)
    return (layer_output, input_grad, gate_grad, up_grad, down_grad)
```

```python
import functools

import jax
import jax.numpy as jnp
from jax import lax
from jax.experimental import pallas as pl
from jax.experimental.pallas import tpu as pltpu
from jax.sharding import PartitionSpec as P

LEN = 64
BF = jnp.bfloat16
F32 = jnp.float32
MESH = pl.DeviceIdType.MESH


def contract(left, right, left_dim, right_dim):
    return lax.dot_general(
        left, right, (((left_dim,), (right_dim,)), ((), ())), preferred_element_type=F32
    )


def kernel(
    x_ref, g_ref, wg_ref, wu_ref, wd_ref, mask_ref,
    out_ref, dx_ref, xg_out, hid_out,
    xg, hid, acc, st_a, st_b, xa, zb, acc_b, acc_a, st_z, za, st_x, xb,
    o_own, sib_st, sib_rx, st_o, o_rx,
    t_ss, t_rs, xa_ss, xa_rs, zb_ss, zb_rs, za_ss, za_rs, xb_ss, xb_rs,
    g_ss, g_rs, s_ss, s_rs, o_ss, o_rs, loc,
):
    dp = lax.axis_index("dp")
    t = lax.axis_index("tensor")
    xl, z = dp // 4, dp % 4
    xh, y, c = t // 8, (t // 2) % 4, t % 2

    def on_dp(xl_, z_):
        return (xl_ * 4 + z_, t)

    def on_tensor(xh_, y_, c_):
        return (dp, (xh_ * 4 + y_) * 2 + c_)

    x_peer = on_dp(1 - xl, z)
    z_peer = [on_dp(xl, (z + r) % 4) for r in range(4)]
    sibling = on_tensor(xh, y, 1 - c)
    chips = [((xh + i // 4) % 2, (y + i % 4) % 4) for i in range(8)]
    from_chips = [((xh + i // 4) % 2, (y + 4 - i % 4) % 4) for i in range(8)]

    def rows(slot, count=1):
        return pl.ds(pl.multiple_of(slot * LEN, LEN), count * LEN)

    def remote(src, dst, ss, rs, dev):
        return pltpu.make_async_remote_copy(
            src_ref=src, dst_ref=dst, send_sem=ss, recv_sem=rs, device_id=dev, device_id_type=MESH
        )

    bar = pltpu.get_barrier_semaphore()
    peers = [x_peer] + z_peer[1:] + [sibling] + [on_tensor(a, b, c) for a, b in chips[1:]]
    for dev in peers:
        pl.semaphore_signal(bar, inc=1, device_id=dev, device_id_type=MESH)

    my_slot = (c * 2 + xh) * 4 + y
    xg[0, rows(my_slot), :] = x_ref[...]
    xg[1, rows(my_slot), :] = g_ref[...]
    pl.semaphore_wait(bar, len(peers))

    pending = []
    mine = xg.at[:, rows(my_slot), :]
    own = []
    for i in range(1, 8):
        a, b = chips[i]
        copy = remote(mine, mine, t_ss.at[i], t_rs.at[i], on_tensor(a, b, c))
        copy.start()
        own.append(copy)
    copy = remote(mine, mine, t_ss.at[0], t_rs.at[0], sibling)
    copy.start()
    own.append(copy)
    shared = []
    for i in range(1, 8):
        own[i - 1].wait_recv()
        a, b = from_chips[i]
        part = xg.at[:, rows((c * 2 + a) * 4 + b), :]
        copy = remote(part, part, t_ss.at[7 + i], t_rs.at[7 + i], sibling)
        copy.start()
        shared.append(copy)
    own[7].wait_recv()
    for copy in shared:
        copy.wait_recv()
    pending += own + shared
    xg_copy = pltpu.make_async_copy(xg, xg_out, loc.at[0])
    xg_copy.start()

    def products(q):
        r4 = pl.ds(pl.multiple_of(q * 256, 256), 256)
        xs = xg[0, r4, :]
        acc[0] = jnp.dot(xs, wg_ref[...], preferred_element_type=F32)
        acc[1] = jnp.dot(xs, wu_ref[...], preferred_element_type=F32)
        acc[2] = contract(xg[1, r4, :], wd_ref[...], 1, 1)

    products(1 - xl)
    for k in range(3):
        st_a[k] = acc[k].astype(BF)
    to_x = []
    for r in (2, 1, 3, 0):
        part = rows((z + r) % 4)
        copy = remote(st_a.at[:, part, :], xa.at[:, part, :], xa_ss.at[r], xa_rs.at[r], x_peer)
        copy.start()
        to_x.append((r, copy))
    to_z = [[None] * 3, [None] * 3]
    for j in range(2):
        side = xl if j else 1 - xl
        products(2 + side)
        for k in range(3):
            st_b[j, k] = acc[k].astype(BF)
            acc_b[j, k] = acc[k, rows(z), :]
        for r in (2, 1, 3):
            copy = remote(
                st_b.at[j, :, rows((z + r) % 4), :], zb.at[j, r - 1],
                zb_ss.at[j * 3 + r - 1], zb_rs.at[j * 3 + r - 1], z_peer[r],
            )
            copy.start()
            to_z[j][r - 1] = copy
    products(xl)
    pairs = []
    for r, copy in to_x:
        copy.wait_recv()
        part = rows((z + r) % 4)
        if r:
            for k in range(3):
                st_z[r - 1, k] = (acc[k, part, :] + xa[k, part, :].astype(F32)).astype(BF)
            pair = remote(st_z.at[r - 1], za.at[r - 1], za_ss.at[r - 1], za_rs.at[r - 1], z_peer[r])
            pair.start()
            pairs.append(pair)
        else:
            for k in range(3):
                acc_a[k] = acc[k, part, :] + xa[k, part, :].astype(F32)
    pending_send = [copy for _, copy in to_x] + to_z[0] + to_z[1] + pairs

    for copy in to_z[0]:
        copy.wait_recv()
    for k in range(3):
        st_x[k] = acc_b[0, k] + (
            zb[0, 0, k].astype(F32) + zb[0, 1, k].astype(F32) + zb[0, 2, k].astype(F32)
        )
    to_xb = remote(st_x, xb, xb_ss.at[0], xb_rs.at[0], x_peer)
    to_xb.start()
    pending_send.append(to_xb)

    def activate(base, parts, extra, which, slot):
        def step(i, carry):
            rr = pl.ds(pl.multiple_of(i * 16, 16), 16)

            def total(k):
                v = base(k, rr)
                for p in range(3):
                    v = v + parts(p, k, rr).astype(F32)
                return v if extra is None else v + extra[k, rr, :]

            gate_pre, up_pre, hidden_grad = total(0), total(1), total(2)
            keep = mask_ref[which]
            sig = jax.nn.sigmoid(gate_pre)
            act = gate_pre * sig
            dst = pl.ds(pl.multiple_of(slot * LEN + i * 16, 16), 16)
            hid[0, dst, :] = (act * up_pre * keep).astype(BF)
            hid[1, dst, :] = (
                hidden_grad * up_pre * sig * (1.0 + gate_pre * (1.0 - sig)) * keep
            ).astype(BF)
            hid[2, dst, :] = (hidden_grad * act * keep).astype(BF)
            return carry

        lax.fori_loop(0, LEN // 16, step, 0)

    def give(slot, sem, dev):
        part = hid.at[:, rows(slot), :]
        copy = remote(part, part, g_ss.at[sem], g_rs.at[sem], dev)
        copy.start()
        pending_send.append(copy)
        return copy

    slot_a, slot_b = 4 * xl + z, 8 + 4 * xl + z
    for copy in pairs:
        copy.wait_recv()
    activate(
        lambda k, rr: acc_a[k, rr, :], lambda p, k, rr: za[p, k, rr, :], None, 0, slot_a
    )
    a_z = {r: give(slot_a, r - 1, z_peer[r]) for r in (2, 1, 3)}
    a_x = {0: give(slot_a, 3, x_peer)}
    for copy in to_z[1]:
        copy.wait_recv()
    to_xb.wait_recv()
    activate(
        lambda k, rr: acc_b[1, k, rr, :], lambda p, k, rr: zb[1, p, k, rr, :], xb, 1, slot_b
    )
    b_x = give(slot_b, 7, x_peer)
    b_z = {r: give(slot_b, 7 + r, z_peer[r]) for r in (2, 1, 3)}
    for r in (1, 3, 2):
        a_z[r].wait_recv()
        a_x[r] = give(4 * xl + (z + 4 - r) % 4, 3 + r, x_peer)
    b_x.wait_recv()
    b_f = {r: give(8 + 4 * (1 - xl) + z, 10 + r, z_peer[r]) for r in (2, 1, 3)}

    hid_copies = []
    o_sends = []

    def outputs(n, core, q, side):
        r4 = pl.ds(pl.multiple_of(q * 256, 256), 256)
        keep = pltpu.make_async_copy(hid.at[:, r4, :], hid_out.at[:, r4, :], loc.at[1 + n])
        keep.start()
        hid_copies.append(keep)
        o = jnp.dot(hid[0, r4, :], wd_ref[...], preferred_element_type=F32)
        d = contract(hid[1, r4, :], wg_ref[...], 1, 1) + contract(hid[2, r4, :], wu_ref[...], 1, 1)
        m = n // 2
        to_sib = remote(sib_st.at[m], sib_rx.at[m], s_ss.at[m], s_rs.at[m], sibling)

        mine_at = jnp.where(c == core, 2, m)
        sib_st[mine_at, 0] = o
        sib_st[mine_at, 1] = d

        @pl.when(c != core)
        def _():
            to_sib.start()

        far = (side + xh) % 2

        @pl.when(c == core)
        def _():
            to_sib.wait_recv()
            for k in range(2):
                st_o[m, k] = (sib_st[2, k] + sib_rx[m, k]).astype(BF)

            @pl.when(far == 0)
            def _():
                for k in range(2):
                    o_own[k] = sib_st[2, k, rows(y), :] + sib_rx[m, k, rows(y), :]

        for r in (2, 1, 3, 0):
            yy = (y + r) % 4
            send = remote(
                st_o.at[m, :, rows(yy), :], o_rx.at[far * 4 + r],
                o_ss.at[m * 4 + r], o_rs.at[far * 4 + r], on_tensor(side, yy, c),
            )
            ok = (c == core) if r else ((c == core) & (far == 1))

            @pl.when(ok)
            def _(send=send):
                send.start()

            o_sends.append((ok, send))
        return (c != core), to_sib

    sib = []
    sib.append(outputs(0, 0, xl, xl))
    for r in (1, 2, 3):
        b_z[r].wait_recv()
    sib.append(outputs(1, 1, 2 + xl, xl))
    for r in (1, 2, 3):
        b_f[r].wait_recv()
    sib.append(outputs(2, 1, 3 - xl, 1 - xl))
    for r in range(4):
        a_x[r].wait_recv()
    sib.append(outputs(3, 0, 1 - xl, 1 - xl))

    for i in range(1, 8):
        remote(st_o.at[0, :, rows(0), :], o_rx.at[i], o_ss.at[0], o_rs.at[i], sibling).wait_recv()
    for k, ref in ((0, out_ref), (1, dx_ref)):
        v = o_own[k]
        for i in range(1, 8):
            v = v + o_rx[i, k].astype(F32)
        ref[...] = v.astype(BF)

    for copy in pending + pending_send:
        copy.wait_send()
    for ok, send in o_sends + sib:
        @pl.when(ok)
        def _(send=send):
            send.wait_send()
    xg_copy.wait()
    for copy in hid_copies:
        copy.wait()


def local(layer_input, gate_weight, up_weight, down_weight, granularity, out_grad):
    feat, cols = gate_weight.shape
    t = lax.axis_index("tensor")
    dp = lax.axis_index("dp")
    tokens = 16 * LEN
    slots = jnp.stack([dp, 8 + dp])
    seqs = ((slots // 4) % 2 * 4 + slots % 4) * 2 + slots // 8
    widths = jnp.left_shift(jnp.int32(2688), jnp.take(granularity, seqs))
    col = t * cols + jnp.arange(cols, dtype=jnp.int32)
    mask = (col[None, None, :] < widths[:, None, None]).astype(F32)

    vm = pl.BlockSpec(memory_space=pltpu.VMEM)
    hbm = pl.BlockSpec(memory_space=pl.ANY)
    seq3 = (3, LEN, cols)
    dma = pltpu.SemaphoreType.DMA
    out, dx, xg, hid = pl.pallas_call(
        kernel,
        out_shape=(
            jax.ShapeDtypeStruct((LEN, feat), BF),
            jax.ShapeDtypeStruct((LEN, feat), BF),
            jax.ShapeDtypeStruct((2, tokens, feat), BF),
            jax.ShapeDtypeStruct((3, tokens, cols), BF),
        ),
        in_specs=[vm] * 6,
        out_specs=(vm, vm, hbm, hbm),
        scratch_shapes=[
            pltpu.VMEM((2, tokens, feat), BF),
            pltpu.VMEM((3, tokens, cols), BF),
            pltpu.VMEM((3, 256, cols), F32),
            pltpu.VMEM((3, 256, cols), BF),
            pltpu.VMEM((2, 3, 256, cols), BF),
            pltpu.VMEM((3, 256, cols), BF),
            pltpu.VMEM((2, 3) + seq3, BF),
            pltpu.VMEM((2,) + seq3, F32),
            pltpu.VMEM(seq3, F32),
            pltpu.VMEM((3,) + seq3, BF),
            pltpu.VMEM((3,) + seq3, BF),
            pltpu.VMEM(seq3, F32),
            pltpu.VMEM(seq3, F32),
            pltpu.VMEM((2, LEN, feat), F32),
            pltpu.VMEM((3, 2, 256, feat), F32),
            pltpu.VMEM((2, 2, 256, feat), F32),
            pltpu.VMEM((2, 2, 256, feat), BF),
            pltpu.VMEM((8, 2, LEN, feat), BF),
            dma((15,)), dma((15,)),
            dma((4,)), dma((4,)),
            dma((6,)), dma((6,)),
            dma((3,)), dma((3,)),
            dma((1,)), dma((1,)),
            dma((14,)), dma((14,)),
            dma((2,)), dma((2,)),
            dma((8,)), dma((8,)),
            dma((5,)),
        ],
        compiler_params=pltpu.CompilerParams(
            collective_id=0, has_side_effects=True, vmem_limit_bytes=62 << 20
        ),
        cost_estimate=pl.CostEstimate(flops=12_000_000_000, bytes_accessed=20_000_000, transcendentals=0),
    )(layer_input, out_grad, gate_weight, up_weight, down_weight, mask)
    down_grad = contract(hid[0], xg[1], 0, 0).astype(BF)
    gate_grad = contract(xg[0], hid[1], 0, 0).astype(BF)
    up_grad = contract(xg[0], hid[2], 0, 0).astype(BF)
    return out, dx, gate_grad, up_grad, down_grad


def solution(mesh):
    in_specs = (
        P("tensor", "dp"),
        P("dp", "tensor"),
        P("dp", "tensor"),
        P("tensor", "dp"),
        P(),
        P("tensor", "dp"),
    )
    out_specs = (
        P("tensor", "dp"),
        P("tensor", "dp"),
        P("dp", "tensor"),
        P("dp", "tensor"),
        P("tensor", "dp"),
    )
    return jax.shard_map(local, mesh=mesh, in_specs=in_specs, out_specs=out_specs, check_vma=False)
```

```python
import jax
import jax.numpy as jnp
from jax import lax
from jax.experimental import pallas as pl
from jax.experimental.pallas import tpu as pltpu
from jax.sharding import PartitionSpec as P

LEN = 64
BF = jnp.bfloat16
F32 = jnp.float32
MESH = pl.DeviceIdType.MESH


def contract(left, right, left_dim, right_dim):
    return lax.dot_general(
        left, right, (((left_dim,), (right_dim,)), ((), ())), preferred_element_type=F32
    )


def kernel(
    gran_ref, x_ref, g_ref, wg_ref, wu_ref, wd_ref,
    out_ref, dx_ref, xg_out, hid_out,
    xg, hid, acc, keep, st_a, xa, st_b, zb, st_c, zc, st_z, za, st_x, xb,
    o_own, sib_st, sib_rx, st_y, y_rx, st_w, w_rx, ss, rs, loc,
):
    cols = wg_ref.shape[1]
    dp = lax.axis_index("dp")
    t = lax.axis_index("tensor")
    xl, z = dp // 4, dp % 4
    xh, y, c = t // 8, (t // 2) % 4, t % 2
    zp, zf, zm = (z + 1) % 4, (z + 2) % 4, (z + 3) % 4

    def on_tensor(xh_, y_, c_):
        return (dp, (xh_ * 4 + y_ % 4) * 2 + c_)

    x_peer = ((1 - xl) * 4 + z, t)
    z_peer = [(xl * 4 + (z + r) % 4, t) for r in range(4)]
    sibling = on_tensor(xh, y, 1 - c)
    far_chip = on_tensor(1 - xh, y, c)
    y_chip = [on_tensor(xh, y + r, c) for r in range(4)]
    y_of = (0, 3, 1, 2)

    sends = []

    def send(src, dst, dev):
        i = len(sends)
        copy = pltpu.make_async_remote_copy(
            src_ref=src, dst_ref=dst, send_sem=ss.at[i], recv_sem=rs.at[i],
            device_id=dev, device_id_type=MESH,
        )
        copy.start()
        sends.append(copy)
        return copy

    def got(*copies):
        for copy in copies:
            copy.wait_recv()

    def r16(i, base=0):
        return pl.ds(pl.multiple_of(base + i * 16, 16), 16)

    def r64(i, base=0):
        return pl.ds(pl.multiple_of(base + i * LEN, LEN), LEN)

    bar = pltpu.get_barrier_semaphore()
    peers = [x_peer, sibling, far_chip] + z_peer[1:] + y_chip[1:]
    for dev in peers:
        pl.semaphore_signal(bar, inc=1, device_id=dev, device_id_type=MESH)
    xg[0, 0:LEN, :] = x_ref[...]
    xg[1, 0:LEN, :] = g_ref[...]
    pl.semaphore_wait(bar, len(peers))

    def seqs(p, k, n=1):
        return xg.at[:, pl.ds(p * 256 + k * LEN, n * LEN), :]

    mine, theirs = seqs(0, 0), seqs(0, 1)
    i_far = send(mine, seqs(0, 1), far_chip)
    i_sib = send(mine, seqs(0, 2), sibling)
    i_y = {1: send(mine, seqs(1, 0), y_chip[1]), 2: send(mine, seqs(2, 0), y_chip[3])}
    i_y[3] = send(mine, seqs(3, 0), y_chip[2])
    got(i_far)
    i_sib2 = send(theirs, seqs(0, 3), sibling)
    i_y2 = {1: send(theirs, seqs(1, 1), y_chip[1]), 2: send(theirs, seqs(2, 1), y_chip[3])}
    i_y2[3] = send(theirs, seqs(3, 1), y_chip[2])
    i_s = {}
    local_copies = []

    def keep_in_hbm(src, dst):
        copy = pltpu.make_async_copy(src, dst, loc.at[len(local_copies)])
        copy.start()
        local_copies.append(copy)

    def gather(p):
        if p == 0:
            got(i_sib, i_sib2)
        else:
            got(i_y[p], i_y2[p])
            i_s[p] = send(seqs(p, 0, 2), seqs(p, 2, 2), sibling)
            got(i_s[p])
        keep_in_hbm(seqs(p, 0, 4), xg_out.at[:, pl.ds(p * 256, 256), :])

    s_a, s_b, s_c, s_z, s_x = {}, {}, {}, {}, {}

    def products(p):
        gather(p)
        xs = xg[0, p * 256 : p * 256 + 256, :]
        gs = xg[1, p * 256 : p * 256 + 256, :]
        acc[0] = jnp.dot(xs, wg_ref[...], preferred_element_type=F32)
        acc[1] = jnp.dot(xs, wu_ref[...], preferred_element_type=F32)
        acc[2] = jnp.dot(gs, wd_ref[...], preferred_element_type=F32)
        for k in range(3):
            st_a[p, k] = acc[k, r64(1 - xl), :].astype(BF)
        s_a[p] = send(st_a.at[p], xa.at[p], x_peer)
        for k in range(3):
            st_b[p, 0, k, 0:16, :] = acc[k, r16(zf, 128), :].astype(BF)
            st_b[p, 0, k, 16:32, :] = acc[k, r16(zp, 192), :].astype(BF)
            st_b[p, 1, k, 0:16, :] = acc[k, r16(zf, 192), :].astype(BF)
            st_b[p, 1, k, 16:32, :] = acc[k, r16(zm, 128), :].astype(BF)
        s_b[p] = (
            send(st_b.at[p, 0], zb.at[p, 0], z_peer[1]),
            send(st_b.at[p, 1], zb.at[p, 1], z_peer[3]),
        )
        for k in range(3):
            keep[p, k, 0:64, :] = acc[k, r64(xl), :]
            keep[p, k, 64:80, :] = acc[k, r16(zp, 128), :]
            keep[p, k, 80:96, :] = acc[k, r16(zm, 192), :]
            keep[p, k, 96:112, :] = acc[k, r16(z, 128), :]
            keep[p, k, 112:128, :] = acc[k, r16(z, 192), :]

    def second(p):
        sent = []
        for d, peer in ((0, z_peer[1]), (1, z_peer[3])):
            got(s_b[p][d])
            for k in range(3):
                st_c[p, d, k] = (
                    keep[p, k, 64 + 16 * d : 80 + 16 * d, :] + zb[p, d, k, 0:16, :].astype(F32)
                ).astype(BF)
            sent.append(send(st_c.at[p, d], zc.at[p, d], peer))
        s_c[p] = sent
        got(s_a[p])
        sent = []
        for r in (2, 1, 3):
            zz = r16((z + r) % 4)
            for k in range(3):
                st_z[p, r - 1, k] = (keep[p, k, zz, :] + xa[p, k, zz, :].astype(F32)).astype(BF)
            sent.append(send(st_z.at[p, r - 1], za.at[p, r - 1], z_peer[r]))
        s_z[p] = sent

    def third(p):
        got(*s_c[p])
        for k in range(3):
            v0 = keep[p, k, 96:112, :] + zc[p, 0, k].astype(F32) + zb[p, 1, k, 16:32, :].astype(F32)
            v1 = keep[p, k, 112:128, :] + zc[p, 1, k].astype(F32) + zb[p, 0, k, 16:32, :].astype(F32)
            st_x[p, k] = jnp.where(xl == 0, v1, v0).astype(BF)
            keep[p, k, 64:80, :] = jnp.where(xl == 0, v0, v1)
        s_x[p] = send(st_x.at[p], xb.at[p], x_peer)

    def activate(p, k, total):
        seq = ((xh + xl) % 2 * 4 + (y + y_of[p]) % 4) * 2 + (c + k // 2) % 2
        level = gran_ref[seq]
        width = jnp.where(
            level == 0, 2688, jnp.where(level == 1, 5376, jnp.where(level == 2, 10752, 21504))
        )
        col = t * cols + lax.broadcasted_iota(jnp.int32, (1, cols), 1)
        mask = jnp.where(col < width, 1.0, 0.0).astype(F32)
        gate_pre, up_pre, hidden_grad = total(0), total(1), total(2)
        sig = jax.nn.sigmoid(gate_pre)
        act = gate_pre * sig
        at = 4 * p + k + xl
        hid[0, at, r16(z), :] = (act * up_pre * mask).astype(BF)
        hid[1, at, r16(z), :] = (
            hidden_grad * up_pre * sig * (1.0 + gate_pre * (1.0 - sig)) * mask
        ).astype(BF)
        hid[2, at, r16(z), :] = (hidden_grad * act * mask).astype(BF)

    h_az, h_ax, h_bx, h_bz, h_bf = {}, {}, {}, {}, {}

    def share(src, dev):
        return send(src, src, dev)

    def owned(p):
        got(*s_z[p])

        def total_a(k):
            v = keep[p, k, r16(z), :] + xa[p, k, r16(z), :].astype(F32)
            for r in range(3):
                v = v + za[p, r, k].astype(F32)
            return v

        activate(p, 0, total_a)
        part = hid.at[:, 4 * p + xl, r16(z), :]
        h_az[p] = [share(part, z_peer[r]) for r in (2, 1, 3)]
        got(s_x[p])
        activate(p, 2, lambda k: keep[p, k, 64:80, :] + xb[p, k].astype(F32))
        h_bx[p] = share(hid.at[:, 4 * p + 2 + xl, r16(z), :], x_peer)

    def spread(p):
        got(h_bx[p])
        part = hid.at[:, pl.ds(4 * p + 2, 2), r16(z), :]
        h_bz[p] = (share(part, z_peer[1]), share(part, z_peer[3]))
        got(*h_az[p])
        h_ax[p] = share(hid.at[:, 4 * p + xl], x_peer)

    def forward(p):
        got(h_bz[p][0])
        one = share(hid.at[:, 4 * p + 2, r16(zm), :], z_peer[1])
        got(h_bz[p][1])
        two = share(hid.at[:, 4 * p + 3, r16(zp), :], z_peer[3])
        h_bf[p] = (one, two)

    s_o, s_y = {}, {}

    def outputs(p):
        got(h_ax[p], *h_bf[p])
        keep_in_hbm(hid.at[:, pl.ds(4 * p, 4)], hid_out.at[:, pl.ds(4 * p, 4)])
        h, gd, ud = (hid[i, 4 * p : 4 * p + 4].reshape(256, cols) for i in range(3))
        o = contract(h, wd_ref[...], 1, 1)
        d = contract(gd, wg_ref[...], 1, 1) + contract(ud, wu_ref[...], 1, 1)
        for i, v in ((0, o), (1, d)):
            sib_st[p, i] = v[128:, :]
            o_own[p % 2, i] = v[:128, :]
        s_o[p] = send(sib_st.at[p], sib_rx.at[p], sibling)

    def between_cores(p):
        got(s_o[p])
        if p == 0:
            o_own[0] = o_own[0] + sib_rx[0]
        else:
            st_y[p - 1] = (o_own[p % 2] + sib_rx[p]).astype(BF)
            s_y[p] = send(st_y.at[p - 1], y_rx.at[p - 1], y_chip[y_of[p]])

    products(0)
    products(1)
    second(0)
    products(2)
    second(1)
    third(0)
    third(1)
    owned(1)
    second(2)
    spread(1)
    products(3)
    third(2)
    forward(1)
    owned(2)
    second(3)
    spread(2)
    outputs(1)
    third(3)
    forward(2)
    between_cores(1)
    owned(3)
    owned(0)
    outputs(2)
    spread(3)
    spread(0)
    between_cores(2)
    forward(3)
    forward(0)
    outputs(3)
    between_cores(3)
    outputs(0)
    between_cores(0)

    got(s_y[1], s_y[2], s_y[3])
    for i in range(2):
        v = o_own[0, i]
        for p in range(3):
            v = v + y_rx[p, i].astype(F32)
        o_own[0, i] = v
        st_w[i] = v[LEN:, :].astype(BF)
    got(send(st_w, w_rx, far_chip))
    out_ref[...] = (o_own[0, 0, 0:LEN, :] + w_rx[0].astype(F32)).astype(BF)
    dx_ref[...] = (o_own[0, 1, 0:LEN, :] + w_rx[1].astype(F32)).astype(BF)

    for copy in sends:
        copy.wait_send()
    for copy in local_copies:
        copy.wait()
    assert len(sends) == N_SENDS


N_SENDS = 12 + 4 * 19 + 3 + 1


def local(layer_input, gate_weight, up_weight, down_weight, granularity, out_grad):
    feat, cols = gate_weight.shape
    vm = pl.BlockSpec(memory_space=pltpu.VMEM)
    hbm = pl.BlockSpec(memory_space=pl.ANY)
    sm = pl.BlockSpec(memory_space=pltpu.SMEM)
    out, dx, xg, hid = pl.pallas_call(
        kernel,
        out_shape=(
            jax.ShapeDtypeStruct((LEN, feat), BF),
            jax.ShapeDtypeStruct((LEN, feat), BF),
            jax.ShapeDtypeStruct((2, 1024, feat), BF),
            jax.ShapeDtypeStruct((3, 16, LEN, cols), BF),
        ),
        in_specs=[sm] + [vm] * 5,
        out_specs=(vm, vm, hbm, hbm),
        scratch_shapes=[
            pltpu.VMEM((2, 1024, feat), BF),
            pltpu.VMEM((3, 16, LEN, cols), BF),
            pltpu.VMEM((3, 256, cols), F32),
            pltpu.VMEM((4, 3, 128, cols), F32),
            pltpu.VMEM((4, 3, LEN, cols), BF),
            pltpu.VMEM((4, 3, LEN, cols), BF),
            pltpu.VMEM((4, 2, 3, 32, cols), BF),
            pltpu.VMEM((4, 2, 3, 32, cols), BF),
            pltpu.VMEM((4, 2, 3, 16, cols), BF),
            pltpu.VMEM((4, 2, 3, 16, cols), BF),
            pltpu.VMEM((4, 3, 3, 16, cols), BF),
            pltpu.VMEM((4, 3, 3, 16, cols), BF),
            pltpu.VMEM((4, 3, 16, cols), BF),
            pltpu.VMEM((4, 3, 16, cols), BF),
            pltpu.VMEM((2, 2, 128, feat), F32),
            pltpu.VMEM((4, 2, 128, feat), F32),
            pltpu.VMEM((4, 2, 128, feat), F32),
            pltpu.VMEM((3, 2, 128, feat), BF),
            pltpu.VMEM((3, 2, 128, feat), BF),
            pltpu.VMEM((2, LEN, feat), BF),
            pltpu.VMEM((2, LEN, feat), BF),
            pltpu.SemaphoreType.DMA((N_SENDS,)),
            pltpu.SemaphoreType.DMA((N_SENDS,)),
            pltpu.SemaphoreType.DMA((8,)),
        ],
        compiler_params=pltpu.CompilerParams(
            collective_id=0, has_side_effects=True, vmem_limit_bytes=62 << 20
        ),
        cost_estimate=pl.CostEstimate(flops=12_000_000_000, bytes_accessed=20_000_000, transcendentals=0),
    )(granularity, layer_input, out_grad, gate_weight, up_weight, down_weight.T)
    hid = hid.reshape(3, 1024, cols)
    down_grad = contract(xg[1], hid[0], 0, 0).astype(BF).T
    gate_grad = contract(xg[0], hid[1], 0, 0).astype(BF)
    up_grad = contract(xg[0], hid[2], 0, 0).astype(BF)
    return out, dx, gate_grad, up_grad, down_grad


def solution(mesh):
    in_specs = (
        P("tensor", "dp"),
        P("dp", "tensor"),
        P("dp", "tensor"),
        P("tensor", "dp"),
        P(),
        P("tensor", "dp"),
    )
    out_specs = (
        P("tensor", "dp"),
        P("tensor", "dp"),
        P("dp", "tensor"),
        P("dp", "tensor"),
        P("tensor", "dp"),
    )
    return jax.shard_map(local, mesh=mesh, in_specs=in_specs, out_specs=out_specs, check_vma=False)
```

```python
import jax
import jax.numpy as jnp
from jax import lax
from jax.experimental import pallas as pl
from jax.experimental.pallas import tpu as pltpu
from jax.sharding import PartitionSpec as P

LEN = 64
BF = jnp.bfloat16
F32 = jnp.float32
MESH = pl.DeviceIdType.MESH


def contract(left, right, left_dim, right_dim):
    return lax.dot_general(
        left, right, (((left_dim,), (right_dim,)), ((), ())), preferred_element_type=F32
    )


def kernel(
    gran_ref, x_ref, g_ref, wg_hbm, wu_hbm, wd_hbm,
    out_ref, dx_ref, gate_out, up_out, down_out,
    wg_ref, wu_ref, wd_ref, xg, hid, pool, st_a, xa, st_b, zb_flat, st_c, zc, st_z, za, st_x, xb,
    o_own, sib_st, sib_rx, st_y, y_rx, st_w, w_rx, ss, rs, loc,
):
    feat, cols = wg_ref.shape
    dp = lax.axis_index("dp")
    t = lax.axis_index("tensor")
    xl, z = dp // 4, dp % 4
    xh, y, c = t // 8, (t // 2) % 4, t % 2
    zp, zf, zm = (z + 1) % 4, (z + 2) % 4, (z + 3) % 4

    def on_tensor(xh_, y_, c_):
        return (dp, (xh_ * 4 + y_ % 4) * 2 + c_)

    x_peer = ((1 - xl) * 4 + z, t)
    z_peer = [(xl * 4 + (z + r) % 4, t) for r in range(4)]
    sibling = on_tensor(xh, y, 1 - c)
    far_chip = on_tensor(1 - xh, y, c)
    y_chip = [on_tensor(xh, y + r, c) for r in range(4)]
    y_of = (0, 3, 1, 2)

    sends = []

    def send(src, dst, dev):
        i = len(sends)
        copy = pltpu.make_async_remote_copy(
            src_ref=src, dst_ref=dst, send_sem=ss.at[i], recv_sem=rs.at[i],
            device_id=dev, device_id_type=MESH,
        )
        copy.start()
        sends.append(copy)
        return copy

    def got(*copies):
        for copy in copies:
            copy.wait_recv()

    def r16(i, base=0):
        return pl.ds(pl.multiple_of(base + i * 16, 16), 16)

    def r64(i, base=0):
        return pl.ds(pl.multiple_of(base + i * LEN, LEN), LEN)

    loads = []
    for i, (src, dst) in enumerate(((wg_hbm, wg_ref), (wu_hbm, wu_ref), (wd_hbm, wd_ref))):
        load = pltpu.make_async_copy(src, dst, loc.at[i])
        load.start()
        loads.append(load)

    bar = pltpu.get_barrier_semaphore()
    peers = [x_peer, sibling, far_chip] + z_peer[1:] + y_chip[1:]
    for dev in peers:
        pl.semaphore_signal(bar, inc=1, device_id=dev, device_id_type=MESH)
    xg[0, 0:LEN, :] = x_ref[...]
    xg[1, 0:LEN, :] = g_ref[...]
    pl.semaphore_wait(bar, len(peers))

    def seqs(p, k, n=1):
        return xg.at[:, pl.ds(p * 256 + k * LEN, n * LEN), :]

    mine, theirs = seqs(0, 0), seqs(0, 1)
    i_far = send(mine, seqs(0, 1), far_chip)
    i_sib = send(mine, seqs(0, 2), sibling)
    i_y = {1: send(mine, seqs(1, 0), y_chip[1]), 2: send(mine, seqs(2, 0), y_chip[3])}
    i_y[3] = send(mine, seqs(3, 0), y_chip[2])
    got(i_far)
    i_sib2 = send(theirs, seqs(0, 3), sibling)
    i_y2 = {1: send(theirs, seqs(1, 1), y_chip[1]), 2: send(theirs, seqs(2, 1), y_chip[3])}
    i_y2[3] = send(theirs, seqs(3, 1), y_chip[2])
    i_s = {}
    def gather(p):
        if p == 0:
            got(i_sib, i_sib2)
        else:
            got(i_y[p], i_y2[p])
            i_s[p] = send(seqs(p, 0, 2), seqs(p, 2, 2), sibling)
            got(i_s[p])

    s_a, s_b, s_c, s_z, s_x = {}, {}, {}, {}, {}

    def acc(k, start, n=16):
        return pl.ds(pl.multiple_of(k * 256 + start, 16), n)

    def keep(p, k, start, n=16):
        return pl.ds(pl.multiple_of(768 + (p * 3 + k) * 128 + start, 16), n)

    def zb(p, d, k, start=0):
        return pl.ds(p * 192 + d * 96 + k * 32 + start, 16)

    def products(p):
        gather(p)
        if p == 0:
            for load in loads:
                load.wait()
        xs = xg[0, p * 256 : p * 256 + 256, :]
        gs = xg[1, p * 256 : p * 256 + 256, :]
        pool[0:256, :] = jnp.dot(xs, wg_ref[...], preferred_element_type=F32)
        pool[256:512, :] = jnp.dot(xs, wu_ref[...], preferred_element_type=F32)
        pool[512:768, :] = jnp.dot(gs, wd_ref[...], preferred_element_type=F32)
        for k in range(3):
            st_a[p * 192 + k * 64 : p * 192 + k * 64 + 64, :] = pool[acc(k, (1 - xl) * 64, 64), :].astype(BF)
        s_a[p] = send(st_a.at[pl.ds(p * 192, 192), :], xa.at[pl.ds(p * 192, 192), :], x_peer)
        for k in range(3):
            st_b[zb(p, 0, k, 0), :] = pool[acc(k, 128 + 16 * zf), :].astype(BF)
            st_b[zb(p, 0, k, 16), :] = pool[acc(k, 192 + 16 * zp), :].astype(BF)
            st_b[zb(p, 1, k, 0), :] = pool[acc(k, 192 + 16 * zf), :].astype(BF)
            st_b[zb(p, 1, k, 16), :] = pool[acc(k, 128 + 16 * zm), :].astype(BF)
        s_b[p] = (
            send(st_b.at[pl.ds(p * 192, 96), :], zb_flat.at[pl.ds(p * 192, 96), :], z_peer[1]),
            send(st_b.at[pl.ds(p * 192 + 96, 96), :], zb_flat.at[pl.ds(p * 192 + 96, 96), :], z_peer[3]),
        )
        for k in range(3):
            pool[keep(p, k, 0, 64), :] = pool[acc(k, xl * 64, 64), :]
            pool[keep(p, k, 64), :] = pool[acc(k, 128 + 16 * zp), :]
            pool[keep(p, k, 80), :] = pool[acc(k, 192 + 16 * zm), :]
            pool[keep(p, k, 96), :] = pool[acc(k, 128 + 16 * z), :]
            pool[keep(p, k, 112), :] = pool[acc(k, 192 + 16 * z), :]

    def from_x(p, k, zz):
        return xa[r16(zz, (p * 3 + k) * 64), :].astype(F32)

    def second(p):
        sent = []
        for d, peer in ((0, z_peer[1]), (1, z_peer[3])):
            got(s_b[p][d])
            for k in range(3):
                st_c[p, d, k] = (
                    pool[keep(p, k, 64 + 16 * d), :] + zb_flat[zb(p, d, k), :].astype(F32)
                ).astype(BF)
            sent.append(send(st_c.at[p, d], zc.at[p, d], peer))
        s_c[p] = sent
        got(s_a[p])
        sent = []
        for r in (2, 1, 3):
            zz = (z + r) % 4
            for k in range(3):
                st_z[p, r - 1, k] = (pool[keep(p, k, 16 * zz), :] + from_x(p, k, zz)).astype(BF)
            sent.append(send(st_z.at[p, r - 1], za.at[p, r - 1], z_peer[r]))
        s_z[p] = sent

    def third(p):
        got(*s_c[p])
        for k in range(3):
            v0 = pool[keep(p, k, 96), :] + zc[p, 0, k].astype(F32) + zb_flat[zb(p, 1, k, 16), :].astype(F32)
            v1 = pool[keep(p, k, 112), :] + zc[p, 1, k].astype(F32) + zb_flat[zb(p, 0, k, 16), :].astype(F32)
            st_x[p, k] = jnp.where(xl == 0, v1, v0).astype(BF)
            pool[keep(p, k, 64), :] = jnp.where(xl == 0, v0, v1)
        s_x[p] = send(st_x.at[p], xb.at[p], x_peer)

    def activate(p, k, total):
        seq = ((xh + xl) % 2 * 4 + (y + y_of[p]) % 4) * 2 + (c + k // 2) % 2
        level = gran_ref[seq]
        width = jnp.where(
            level == 0, 2688, jnp.where(level == 1, 5376, jnp.where(level == 2, 10752, 21504))
        )
        col = t * cols + lax.broadcasted_iota(jnp.int32, (1, cols), 1)
        mask = jnp.where(col < width, 1.0, 0.0).astype(F32)
        gate_pre, up_pre, hidden_grad = total(0), total(1), total(2)
        sig = jax.nn.sigmoid(gate_pre)
        act = gate_pre * sig
        at = 4 * p + k + xl
        hid[0, at, r16(z), :] = (act * up_pre * mask).astype(BF)
        hid[1, at, r16(z), :] = (
            hidden_grad * up_pre * sig * (1.0 + gate_pre * (1.0 - sig)) * mask
        ).astype(BF)
        hid[2, at, r16(z), :] = (hidden_grad * act * mask).astype(BF)

    h_az, h_ax, h_bx, h_bz, h_bf = {}, {}, {}, {}, {}

    def share(src, dev):
        return send(src, src, dev)

    def owned(p):
        got(*s_z[p])

        def total_a(k):
            v = pool[keep(p, k, 16 * z), :] + from_x(p, k, z)
            for r in range(3):
                v = v + za[p, r, k].astype(F32)
            return v

        activate(p, 0, total_a)
        part = hid.at[:, 4 * p + xl, r16(z), :]
        h_az[p] = {r: share(part, z_peer[r]) for r in (2, 1, 3)}
        h_ax[p] = [share(part, x_peer)]
        got(s_x[p])
        activate(p, 2, lambda k: pool[keep(p, k, 64), :] + xb[p, k].astype(F32))
        h_bx[p] = share(hid.at[:, 4 * p + 2 + xl, r16(z), :], x_peer)

    def spread(p):
        got(h_bx[p])
        part = hid.at[:, pl.ds(4 * p + 2, 2), r16(z), :]
        h_bz[p] = (share(part, z_peer[1]), share(part, z_peer[3]))
        for r in (1, 3, 2):
            got(h_az[p][r])
            h_ax[p].append(share(hid.at[:, 4 * p + xl, r16((z + 4 - r) % 4), :], x_peer))

    def forward(p):
        got(h_bz[p][0])
        one = share(hid.at[:, 4 * p + 2, r16(zm), :], z_peer[1])
        got(h_bz[p][1])
        two = share(hid.at[:, 4 * p + 3, r16(zp), :], z_peer[3])
        h_bf[p] = (one, two)

    s_o, s_y = {}, {}

    def output_rows(p, first, n):
        seq = 4 * p + first // LEN
        h, gd, ud = (hid[i, seq : seq + n // LEN].reshape(n, cols) for i in range(3))
        o = contract(h, wd_ref[...], 1, 1)
        return o, contract(gd, wg_ref[...], 1, 1) + contract(ud, wu_ref[...], 1, 1)

    def outputs(p):
        got(*h_ax[p], *h_bf[p])
        for i, v in enumerate(output_rows(p, 0, 256)):
            sib_st[p, i] = v[128:, :]
            o_own[p % 2, i] = v[:128, :]
        s_o[p] = send(sib_st.at[p], sib_rx.at[p], sibling)

    def outputs_in_halves(p):
        got(*h_bf[p])
        for i, v in enumerate(output_rows(p, 128, 128)):
            sib_st[p, i] = v
        s_o[p] = send(sib_st.at[p], sib_rx.at[p], sibling)
        got(*h_ax[p])
        for i, v in enumerate(output_rows(p, 0, 128)):
            o_own[p % 2, i] = v

    grads = ((1, down_out, st_a), (0, gate_out, xa), (0, up_out, zb_flat))
    stores = []

    def weight_grads(n, p, rounds, last=False):
        side, dst, stage = grads[n]
        right = hid[n, 4 * p : 4 * (p + rounds)].reshape(256 * rounds, cols)
        for i in range(0, feat, 256):
            size = min(256, feat - i)
            left = xg[side, 256 * p : 256 * (p + rounds), i : i + size]
            v = contract(left, right, 0, 0)
            at = slice(n * feat + i, n * feat + i + size)
            if rounds == 1:
                v = pool[at, :] + v
            if last:
                stage[i : i + size, :] = v.astype(BF)
            else:
                pool[at, :] = v
        if last:
            copy = pltpu.make_async_copy(stage.at[pl.ds(0, feat), :], dst, loc.at[3 + n])
            copy.start()
            stores.append(copy)

    def between_cores(p):
        got(s_o[p])
        if p == 0:
            o_own[0] = o_own[0] + sib_rx[0]
        else:
            st_y[p - 1] = (o_own[p % 2] + sib_rx[p]).astype(BF)
            s_y[p] = send(st_y.at[p - 1], y_rx.at[p - 1], y_chip[y_of[p]])

    products(0)
    products(1)
    second(0)
    products(2)
    second(1)
    third(0)
    third(1)
    owned(1)
    second(2)
    spread(1)
    products(3)
    third(2)
    forward(1)
    owned(2)
    second(3)
    spread(2)
    outputs(1)
    third(3)
    forward(2)
    between_cores(1)
    owned(3)
    outputs(2)
    spread(3)
    owned(0)
    between_cores(2)
    weight_grads(0, 1, 2)
    forward(3)
    spread(0)
    weight_grads(1, 1, 2)
    outputs(3)
    weight_grads(2, 1, 2)
    between_cores(3)
    forward(0)
    weight_grads(0, 3, 1)
    weight_grads(1, 3, 1)
    weight_grads(2, 3, 1)
    outputs_in_halves(0)
    between_cores(0)

    got(s_y[1], s_y[2], s_y[3])
    for i in range(2):
        v = o_own[0, i]
        for p in range(3):
            v = v + y_rx[p, i].astype(F32)
        o_own[0, i] = v
        st_w[i] = v[LEN:, :].astype(BF)
    last = send(st_w, w_rx, far_chip)
    for copy in s_a.values():
        copy.wait_send()
    for n in range(3):
        weight_grads(n, 0, 1, True)
    got(last)
    out_ref[...] = (o_own[0, 0, 0:LEN, :] + w_rx[0].astype(F32)).astype(BF)
    dx_ref[...] = (o_own[0, 1, 0:LEN, :] + w_rx[1].astype(F32)).astype(BF)

    for copy in sends:
        if all(copy is not early for early in s_a.values()):
            copy.wait_send()
    for copy in stores:
        copy.wait()
    assert len(sends) == N_SENDS


N_SENDS = 12 + 4 * 22 + 3 + 1


def move(*refs):
    loads, stores = refs[-2], refs[-1]
    n = loads.shape[0]
    reads = [
        pltpu.make_async_copy(refs[i], refs[2 * n + i], loads.at[i]) for i in range(n)
    ]
    writes = [
        pltpu.make_async_copy(refs[2 * n + i], refs[n + i], stores.at[i]) for i in range(n)
    ]
    for copy in reads:
        copy.start()
    for read, write in zip(reads, writes):
        read.wait()
        write.start()
    for copy in writes:
        copy.wait()


def local(layer_input, gate_weight, up_weight, down_weight, granularity, out_grad):
    feat, cols = gate_weight.shape
    vm = pl.BlockSpec(memory_space=pltpu.VMEM)
    hbm = pl.BlockSpec(memory_space=pl.ANY)
    sm = pl.BlockSpec(memory_space=pltpu.SMEM)
    side = jax.ShapeDtypeStruct((LEN, feat), BF)
    weight = jax.ShapeDtypeStruct((feat, cols), BF)
    results = (side, side, weight, weight, weight)
    parts = pl.pallas_call(
        kernel,
        out_shape=results,
        in_specs=[sm, vm, vm, hbm, hbm, hbm],
        out_specs=(vm, vm, hbm, hbm, hbm),
        scratch_shapes=[
            pltpu.VMEM((feat, cols), BF),
            pltpu.VMEM((feat, cols), BF),
            pltpu.VMEM((feat, cols), BF),
            pltpu.VMEM((2, 1024, feat), BF),
            pltpu.VMEM((3, 16, LEN, cols), BF),
            pltpu.VMEM((768 + 4 * 3 * 128, cols), F32),
            pltpu.VMEM((4 * 3 * LEN, cols), BF),
            pltpu.VMEM((4 * 3 * LEN, cols), BF),
            pltpu.VMEM((4 * 2 * 3 * 32, cols), BF),
            pltpu.VMEM((4 * 2 * 3 * 32, cols), BF),
            pltpu.VMEM((4, 2, 3, 16, cols), BF),
            pltpu.VMEM((4, 2, 3, 16, cols), BF),
            pltpu.VMEM((4, 3, 3, 16, cols), BF),
            pltpu.VMEM((4, 3, 3, 16, cols), BF),
            pltpu.VMEM((4, 3, 16, cols), BF),
            pltpu.VMEM((4, 3, 16, cols), BF),
            pltpu.VMEM((2, 2, 128, feat), F32),
            pltpu.VMEM((4, 2, 128, feat), F32),
            pltpu.VMEM((4, 2, 128, feat), F32),
            pltpu.VMEM((3, 2, 128, feat), BF),
            pltpu.VMEM((3, 2, 128, feat), BF),
            pltpu.VMEM((2, LEN, feat), BF),
            pltpu.VMEM((2, LEN, feat), BF),
            pltpu.SemaphoreType.DMA((N_SENDS,)),
            pltpu.SemaphoreType.DMA((N_SENDS,)),
            pltpu.SemaphoreType.DMA((6,)),
        ],
        compiler_params=pltpu.CompilerParams(
            collective_id=0, has_side_effects=True, vmem_limit_bytes=62 << 20
        ),
        cost_estimate=pl.CostEstimate(flops=17_000_000_000, bytes_accessed=20_000_000, transcendentals=0),
    )(granularity, layer_input, out_grad, gate_weight, up_weight, down_weight.T)
    out, dx, gate_grad, up_grad, down_grad = pl.pallas_call(
        move,
        out_shape=results,
        in_specs=[hbm] * 5,
        out_specs=(hbm,) * 5,
        scratch_shapes=[pltpu.VMEM(r.shape, BF) for r in results]
        + [pltpu.SemaphoreType.DMA((5,))] * 2,
        compiler_params=pltpu.CompilerParams(vmem_limit_bytes=62 << 20),
        cost_estimate=pl.CostEstimate(flops=0, bytes_accessed=11_000_000, transcendentals=0),
    )(*parts)
    return out, dx, gate_grad, up_grad, down_grad.T


def solution(mesh):
    in_specs = (
        P("tensor", "dp"),
        P("dp", "tensor"),
        P("dp", "tensor"),
        P("tensor", "dp"),
        P(),
        P("tensor", "dp"),
    )
    out_specs = (
        P("tensor", "dp"),
        P("tensor", "dp"),
        P("dp", "tensor"),
        P("dp", "tensor"),
        P("tensor", "dp"),
    )
    return jax.shard_map(local, mesh=mesh, in_specs=in_specs, out_specs=out_specs, check_vma=False)
```

```python
import jax
import jax.numpy as jnp
from jax import lax
from jax.experimental import pallas as pl
from jax.experimental.pallas import tpu as pltpu
from jax.sharding import PartitionSpec as P

LEN = 64
BF = jnp.bfloat16
F32 = jnp.float32
MESH = pl.DeviceIdType.MESH


def contract(left, right, left_dim, right_dim):
    return lax.dot_general(
        left, right, (((left_dim,), (right_dim,)), ((), ())), preferred_element_type=F32
    )


def kernel(
    gran_ref, x_ref, g_ref, wg_hbm, wu_hbm, wd_hbm,
    out_ref, dx_ref, gate_out, up_out, down_out,
    wg_ref, wu_ref, wd_ref, ends, xg, hid, pool, pool_end, stage, st_a, xa, st_b, zb, st_c, zc, st_z, za, st_x, xb,
    o_own, sib_st, sib_rx, st_y, y_rx, st_w, w_rx, ss, rs, loc,
):
    feat, cols = wg_ref.shape
    dp = lax.axis_index("dp")
    t = lax.axis_index("tensor")
    xl, z = dp // 4, dp % 4
    xh, y, c = t // 8, (t // 2) % 4, t % 2
    zp, zf, zm = (z + 1) % 4, (z + 2) % 4, (z + 3) % 4

    def on_tensor(xh_, y_, c_):
        return (dp, (xh_ * 4 + y_ % 4) * 2 + c_)

    x_peer = ((1 - xl) * 4 + z, t)
    z_peer = [(xl * 4 + (z + r) % 4, t) for r in range(4)]
    sibling = on_tensor(xh, y, 1 - c)
    far_chip = on_tensor(1 - xh, y, c)
    y_chip = [on_tensor(xh, y + r, c) for r in range(4)]
    y_of = (0, 3, 1, 2)

    sends = []

    def send(src, dst, dev):
        i = len(sends)
        copy = pltpu.make_async_remote_copy(
            src_ref=src, dst_ref=dst, send_sem=ss.at[i], recv_sem=rs.at[i],
            device_id=dev, device_id_type=MESH,
        )
        copy.start()
        sends.append(copy)
        return copy

    def got(*copies):
        for copy in copies:
            copy.wait_recv()

    def r16(i, base=0):
        return pl.ds(pl.multiple_of(base + i * 16, 16), 16)

    def r64(i, base=0):
        return pl.ds(pl.multiple_of(base + i * LEN, LEN), LEN)

    loads = []
    for i, (src, dst) in enumerate(((wg_hbm, wg_ref), (wu_hbm, wu_ref), (wd_hbm, wd_ref))):
        load = pltpu.make_async_copy(src, dst, loc.at[i])
        load.start()
        loads.append(load)

    bar = pltpu.get_barrier_semaphore()
    peers = [x_peer, sibling, far_chip] + z_peer[1:] + y_chip[1:]
    for dev in peers:
        pl.semaphore_signal(bar, inc=1, device_id=dev, device_id_type=MESH)
    xg[0, 0:LEN, :] = x_ref[...]
    xg[1, 0:LEN, :] = g_ref[...]
    pl.semaphore_wait(bar, len(peers))

    def seqs(p, k, n=1):
        return xg.at[:, pl.ds(p * 256 + k * LEN, n * LEN), :]

    mine, theirs = seqs(0, 0), seqs(0, 1)
    i_far = send(mine, seqs(0, 1), far_chip)
    i_sib = send(mine, seqs(0, 2), sibling)
    i_y = {1: send(mine, seqs(1, 0), y_chip[1]), 2: send(mine, seqs(2, 0), y_chip[3])}
    i_y[3] = send(mine, seqs(3, 0), y_chip[2])
    got(i_far)
    i_sib2 = send(theirs, seqs(0, 3), sibling)
    i_y2 = {1: send(theirs, seqs(1, 1), y_chip[1]), 2: send(theirs, seqs(2, 1), y_chip[3])}
    i_y2[3] = send(theirs, seqs(3, 1), y_chip[2])
    i_s = {}
    def gather(p):
        if p == 0:
            got(i_sib, i_sib2)
        else:
            got(i_y[p], i_y2[p])
            i_s[p] = send(seqs(p, 0, 2), seqs(p, 2, 2), sibling)
            got(i_s[p])

    s_a, s_b, s_c, s_z, s_x = {}, {}, {}, {}, {}

    lane = lax.broadcasted_iota(jnp.int32, (1, 128), 1)

    def first_half(v):
        return jnp.where(lane < 64, v, 0.0)

    def acc(start, n=16):
        return pl.ds(pl.multiple_of(start, 16), n)

    def keep(p, start, n=16):
        return pl.ds(pl.multiple_of(256 + p * 128 + start, 16), n)

    def products(p):
        gather(p)
        if p == 0:
            for load in loads:
                load.wait()
            g_end, u_end, d_end = (
                jnp.concatenate([w[:, MAIN:].astype(F32), jnp.zeros((feat, 64), F32)], 1)
                for w in (wg_ref, wu_ref, wd_ref)
            )
            ends[0] = (g_end + pltpu.roll(u_end, 64, 1)).astype(BF)
            ends[1] = d_end.astype(BF)
            ends[2] = pltpu.roll(g_end, 64, 1).astype(BF)
            ends[3] = u_end.astype(BF)
        xs = xg[0, p * 256 : p * 256 + 256, :]
        gs = xg[1, p * 256 : p * 256 + 256, :]
        for at, left, right in (
            (0, xs, wg_ref[:, :MAIN]),
            (MAIN, xs, wu_ref[:, :MAIN]),
            (2 * MAIN, gs, wd_ref[:, :MAIN]),
            (3 * MAIN, xs, ends[0]),
            (3 * MAIN + 128, gs, ends[1]),
        ):
            pool[0:256, at : at + right.shape[1]] = jnp.dot(left, right, preferred_element_type=F32)
        st_a[p] = pool[acc((1 - xl) * 64, 64), :].astype(BF)
        s_a[p] = send(st_a.at[p], xa.at[p], x_peer)
        st_b[p, 0, 0:16, :] = pool[acc(128 + 16 * zf), :].astype(BF)
        st_b[p, 0, 16:32, :] = pool[acc(192 + 16 * zp), :].astype(BF)
        st_b[p, 1, 0:16, :] = pool[acc(192 + 16 * zf), :].astype(BF)
        st_b[p, 1, 16:32, :] = pool[acc(128 + 16 * zm), :].astype(BF)
        s_b[p] = (
            send(st_b.at[p, 0], zb.at[p, 0], z_peer[1]),
            send(st_b.at[p, 1], zb.at[p, 1], z_peer[3]),
        )
        pool[keep(p, 0, 64), :] = pool[acc(xl * 64, 64), :]
        pool[keep(p, 64), :] = pool[acc(128 + 16 * zp), :]
        pool[keep(p, 80), :] = pool[acc(192 + 16 * zm), :]
        pool[keep(p, 96), :] = pool[acc(128 + 16 * z), :]
        pool[keep(p, 112), :] = pool[acc(192 + 16 * z), :]

    def second(p):
        sent = []
        for d, peer in ((0, z_peer[1]), (1, z_peer[3])):
            got(s_b[p][d])
            st_c[p, d] = (
                pool[keep(p, 64 + 16 * d), :] + zb[p, d, 0:16, :].astype(F32)
            ).astype(BF)
            sent.append(send(st_c.at[p, d], zc.at[p, d], peer))
        s_c[p] = sent
        got(s_a[p])
        sent = []
        for r in (2, 1, 3):
            zz = (z + r) % 4
            st_z[p, r - 1] = (
                pool[keep(p, 16 * zz), :] + xa[p, r16(zz), :].astype(F32)
            ).astype(BF)
            sent.append(send(st_z.at[p, r - 1], za.at[p, r - 1], z_peer[r]))
        s_z[p] = sent

    def third(p):
        got(*s_c[p])
        v0 = pool[keep(p, 96), :] + zc[p, 0].astype(F32) + zb[p, 1, 16:32, :].astype(F32)
        v1 = pool[keep(p, 112), :] + zc[p, 1].astype(F32) + zb[p, 0, 16:32, :].astype(F32)
        st_x[p] = jnp.where(xl == 0, v1, v0).astype(BF)
        pool[keep(p, 64), :] = jnp.where(xl == 0, v0, v1)
        s_x[p] = send(st_x.at[p], xb.at[p], x_peer)

    def activate(p, k, total):
        seq = ((xh + xl) % 2 * 4 + (y + y_of[p]) % 4) * 2 + (c + k // 2) % 2
        level = gran_ref[seq]
        width = jnp.where(
            level == 0, 2688, jnp.where(level == 1, 5376, jnp.where(level == 2, 10752, 21504))
        )

        def pointwise(gate_pre, up_pre, hidden_grad, first_col):
            n = gate_pre.shape[1]
            col = t * cols + first_col + lax.broadcasted_iota(jnp.int32, (1, n), 1)
            mask = jnp.where(col < width, 1.0, 0.0).astype(F32)
            sig = jax.nn.sigmoid(gate_pre)
            act = gate_pre * sig
            gate_delta = hidden_grad * up_pre * sig * (1.0 + gate_pre * (1.0 - sig)) * mask
            return act * up_pre * mask, gate_delta, hidden_grad * act * mask

        at = 4 * p + k + xl
        main = pointwise(total(0, MAIN), total(MAIN, MAIN), total(2 * MAIN, MAIN), 0)
        for i, v in enumerate(main):
            hid[at, r16(z), i * MAIN : (i + 1) * MAIN] = v.astype(BF)
        both = total(3 * MAIN, 128)
        gate_end, up_end = first_half(both), first_half(pltpu.roll(both, 64, 1))
        h, gd, ud = pointwise(gate_end, up_end, total(3 * MAIN + 128, 128), MAIN)
        end = first_half(h) + pltpu.roll(first_half(gd), 64, 1)
        hid[at, r16(z), 3 * MAIN : 3 * MAIN + 128] = end.astype(BF)
        hid[at, r16(z), 3 * MAIN + 128 :] = first_half(ud).astype(BF)

    h_az, h_ax, h_bx, h_bz, h_bf = {}, {}, {}, {}, {}

    def share(src, dev):
        return send(src, src, dev)

    def owned(p):
        got(*s_z[p])

        def total_a(at, n):
            v = pool[keep(p, 16 * z), at : at + n] + xa[p, r16(z), at : at + n].astype(F32)
            for r in range(3):
                v = v + za[p, r, :, at : at + n].astype(F32)
            return v

        def total_b(at, n):
            return pool[keep(p, 64), at : at + n] + xb[p, :, at : at + n].astype(F32)

        activate(p, 0, total_a)
        part = hid.at[4 * p + xl, r16(z), :]
        h_az[p] = {r: share(part, z_peer[r]) for r in (2, 1, 3)}
        h_ax[p] = [share(part, x_peer)]
        got(s_x[p])
        activate(p, 2, total_b)
        h_bx[p] = share(hid.at[4 * p + 2 + xl, r16(z), :], x_peer)

    def spread(p):
        got(h_bx[p])
        part = hid.at[pl.ds(4 * p + 2, 2), r16(z), :]
        h_bz[p] = (share(part, z_peer[1]), share(part, z_peer[3]))
        for r in (1, 3, 2):
            got(h_az[p][r])
            h_ax[p].append(share(hid.at[4 * p + xl, r16((z + 4 - r) % 4), :], x_peer))

    def forward(p):
        got(h_bz[p][0])
        one = share(hid.at[4 * p + 2, r16(zm), :], z_peer[1])
        got(h_bz[p][1])
        two = share(hid.at[4 * p + 3, r16(zp), :], z_peer[3])
        h_bf[p] = (one, two)

    s_o, s_y = {}, {}

    def output_rows(p, first, n):
        seq = 4 * p + first // LEN

        def part(at, size=MAIN):
            return hid[seq : seq + n // LEN, :, at : at + size].reshape(n, size)

        o = contract(part(0), wd_ref[:, :MAIN], 1, 1) + contract(part(3 * MAIN, 128), ends[1], 1, 1)
        d = contract(part(MAIN), wg_ref[:, :MAIN], 1, 1)
        d = d + contract(part(2 * MAIN), wu_ref[:, :MAIN], 1, 1)
        d = d + contract(part(3 * MAIN, 128), ends[2], 1, 1)
        return o, d + contract(part(3 * MAIN + 128, 128), ends[3], 1, 1)

    def outputs(p):
        got(*h_ax[p], *h_bf[p])
        for i, v in enumerate(output_rows(p, 0, 256)):
            sib_st[p, i] = v[128:, :]
            o_own[p % 2, i] = v[:128, :]
        s_o[p] = send(sib_st.at[p], sib_rx.at[p], sibling)

    def outputs_in_halves(p):
        got(*h_bf[p])
        for i, v in enumerate(output_rows(p, 128, 128)):
            sib_st[p, i] = v
        s_o[p] = send(sib_st.at[p], sib_rx.at[p], sibling)
        got(*h_ax[p])
        for i, v in enumerate(output_rows(p, 0, 128)):
            o_own[p % 2, i] = v

    grads = (
        ((1, 0, MAIN, pool), (1, 3 * MAIN, 128, pool_end)),
        ((0, MAIN, MAIN, pool),),
        ((0, 2 * MAIN, MAIN, pool), (0, 3 * MAIN, 256, pool)),
    )
    stores = []

    def weight_grads(n, p, rounds):
        for side, at, size, total in grads[n]:
            right = hid[4 * p : 4 * (p + rounds), :, at : at + size].reshape(256 * rounds, size)
            where = 0 if total is pool_end else at
            for i in range(0, feat, 256):
                rows = slice(i, min(i + 256, feat))
                left = xg[side, 256 * p : 256 * (p + rounds), rows]
                v = contract(left, right, 0, 0)
                if rounds == 1:
                    v = total[rows, where : where + size] + v
                total[rows, where : where + size] = v

    def finish_grads(n, dst):
        stage[n, :, 0:MAIN] = pool[0:feat, n * MAIN : (n + 1) * MAIN].astype(BF)
        if n == 0:
            end = pool_end[...]
        elif n == 1:
            end = pltpu.roll(pool[0:feat, 3 * MAIN : 3 * MAIN + 128], 64, 1)
        else:
            end = pool[0:feat, 3 * MAIN + 128 :]
        stage[n, :, MAIN:] = end[:, 0:64].astype(BF)
        copy = pltpu.make_async_copy(stage.at[n], dst, loc.at[3 + n])
        copy.start()
        stores.append(copy)

    def between_cores(p):
        got(s_o[p])
        if p == 0:
            o_own[0] = o_own[0] + sib_rx[0]
        else:
            st_y[p - 1] = (o_own[p % 2] + sib_rx[p]).astype(BF)
            s_y[p] = send(st_y.at[p - 1], y_rx.at[p - 1], y_chip[y_of[p]])

    products(0)
    products(1)
    second(0)
    products(2)
    second(1)
    third(0)
    third(1)
    owned(1)
    second(2)
    spread(1)
    products(3)
    third(2)
    forward(1)
    owned(2)
    second(3)
    spread(2)
    outputs(1)
    third(3)
    forward(2)
    between_cores(1)
    owned(3)
    outputs(2)
    spread(3)
    owned(0)
    between_cores(2)
    weight_grads(0, 1, 2)
    forward(3)
    spread(0)
    weight_grads(1, 1, 2)
    outputs(3)
    weight_grads(2, 1, 2)
    between_cores(3)
    forward(0)
    weight_grads(0, 3, 1)
    weight_grads(1, 3, 1)
    weight_grads(2, 3, 1)
    outputs_in_halves(0)
    between_cores(0)

    got(s_y[1], s_y[2], s_y[3])
    for i in range(2):
        v = o_own[0, i]
        for p in range(3):
            v = v + y_rx[p, i].astype(F32)
        o_own[0, i] = v
        st_w[i] = v[LEN:, :].astype(BF)
    last = send(st_w, w_rx, far_chip)
    for n, dst in ((0, down_out), (2, up_out), (1, gate_out)):
        weight_grads(n, 0, 1)
        finish_grads(n, dst)
    got(last)
    out_ref[...] = (o_own[0, 0, 0:LEN, :] + w_rx[0].astype(F32)).astype(BF)
    dx_ref[...] = (o_own[0, 1, 0:LEN, :] + w_rx[1].astype(F32)).astype(BF)

    for copy in sends:
        copy.wait_send()
    for copy in stores:
        copy.wait()
    assert len(sends) == N_SENDS


MAIN = 1280
WIDE = 4096
N_SENDS = 12 + 4 * 22 + 3 + 1


def move(*refs):
    loads, stores = refs[-2], refs[-1]
    n = loads.shape[0]
    reads = [
        pltpu.make_async_copy(refs[i], refs[2 * n + i], loads.at[i]) for i in range(n)
    ]
    writes = [
        pltpu.make_async_copy(refs[2 * n + i], refs[n + i], stores.at[i]) for i in range(n)
    ]
    for copy in reads:
        copy.start()
    for read, write in zip(reads, writes):
        read.wait()
        write.start()
    for copy in writes:
        copy.wait()


def local(layer_input, gate_weight, up_weight, down_weight, granularity, out_grad):
    feat, cols = gate_weight.shape
    vm = pl.BlockSpec(memory_space=pltpu.VMEM)
    hbm = pl.BlockSpec(memory_space=pl.ANY)
    sm = pl.BlockSpec(memory_space=pltpu.SMEM)
    side = jax.ShapeDtypeStruct((LEN, feat), BF)
    weight = jax.ShapeDtypeStruct((feat, cols), BF)
    results = (side, side, weight, weight, weight)
    parts = pl.pallas_call(
        kernel,
        out_shape=results,
        in_specs=[sm, vm, vm, hbm, hbm, hbm],
        out_specs=(vm, vm, hbm, hbm, hbm),
        scratch_shapes=[
            pltpu.VMEM((feat, cols), BF),
            pltpu.VMEM((feat, cols), BF),
            pltpu.VMEM((feat, cols), BF),
            pltpu.VMEM((4, feat, 128), BF),
            pltpu.VMEM((2, 1024, feat), BF),
            pltpu.VMEM((16, LEN, WIDE), BF),
            pltpu.VMEM((256 + 4 * 128, WIDE), F32),
            pltpu.VMEM((feat, 128), F32),
            pltpu.VMEM((3, feat, cols), BF),
            pltpu.VMEM((4, LEN, WIDE), BF),
            pltpu.VMEM((4, LEN, WIDE), BF),
            pltpu.VMEM((4, 2, 32, WIDE), BF),
            pltpu.VMEM((4, 2, 32, WIDE), BF),
            pltpu.VMEM((4, 2, 16, WIDE), BF),
            pltpu.VMEM((4, 2, 16, WIDE), BF),
            pltpu.VMEM((4, 3, 16, WIDE), BF),
            pltpu.VMEM((4, 3, 16, WIDE), BF),
            pltpu.VMEM((4, 16, WIDE), BF),
            pltpu.VMEM((4, 16, WIDE), BF),
            pltpu.VMEM((2, 2, 128, feat), F32),
            pltpu.VMEM((4, 2, 128, feat), F32),
            pltpu.VMEM((4, 2, 128, feat), F32),
            pltpu.VMEM((3, 2, 128, feat), BF),
            pltpu.VMEM((3, 2, 128, feat), BF),
            pltpu.VMEM((2, LEN, feat), BF),
            pltpu.VMEM((2, LEN, feat), BF),
            pltpu.SemaphoreType.DMA((N_SENDS,)),
            pltpu.SemaphoreType.DMA((N_SENDS,)),
            pltpu.SemaphoreType.DMA((6,)),
        ],
        compiler_params=pltpu.CompilerParams(
            collective_id=0, has_side_effects=True, vmem_limit_bytes=62 << 20
        ),
        cost_estimate=pl.CostEstimate(flops=17_000_000_000, bytes_accessed=20_000_000, transcendentals=0),
    )(granularity, layer_input, out_grad, gate_weight, up_weight, down_weight.T)
    out, dx, gate_grad, up_grad, down_grad = pl.pallas_call(
        move,
        out_shape=results,
        in_specs=[hbm] * 5,
        out_specs=(hbm,) * 5,
        scratch_shapes=[pltpu.VMEM(r.shape, BF) for r in results]
        + [pltpu.SemaphoreType.DMA((5,))] * 2,
        compiler_params=pltpu.CompilerParams(vmem_limit_bytes=62 << 20),
        cost_estimate=pl.CostEstimate(flops=0, bytes_accessed=11_000_000, transcendentals=0),
    )(*parts)
    return out, dx, gate_grad, up_grad, down_grad.T


def solution(mesh):
    in_specs = (
        P("tensor", "dp"),
        P("dp", "tensor"),
        P("dp", "tensor"),
        P("tensor", "dp"),
        P(),
        P("tensor", "dp"),
    )
    out_specs = (
        P("tensor", "dp"),
        P("tensor", "dp"),
        P("dp", "tensor"),
        P("dp", "tensor"),
        P("tensor", "dp"),
    )
    return jax.shard_map(local, mesh=mesh, in_specs=in_specs, out_specs=out_specs, check_vma=False)
```

```python
import jax
import jax.numpy as jnp
from jax import lax
from jax.experimental import pallas as pl
from jax.experimental.pallas import tpu as pltpu
from jax.sharding import PartitionSpec as P

LEN = 64
BF = jnp.bfloat16
F32 = jnp.float32
MESH = pl.DeviceIdType.MESH


def contract(left, right, left_dim, right_dim):
    return lax.dot_general(
        left, right, (((left_dim,), (right_dim,)), ((), ())), preferred_element_type=F32
    )


def kernel(
    gran_ref, x_ref, g_ref, wg_hbm, wu_hbm, wd_hbm,
    out_ref, dx_ref, gate_out, up_out, down_out,
    wg_ref, wu_ref, wd_ref, ends, xg, hid, pool, pool_end, stage, st_a, xa, st_b, zb, st_c, zc, st_z, za, st_x, xb,
    o_own, sib_st, sib_rx, st_y, y_rx, st_w, w_rx, ss, rs, loc,
):
    feat, cols = wg_ref.shape
    dp = lax.axis_index("dp")
    t = lax.axis_index("tensor")
    xl, z = dp // 4, dp % 4
    xh, y, c = t // 8, (t // 2) % 4, t % 2
    zp, zf, zm = (z + 1) % 4, (z + 2) % 4, (z + 3) % 4

    def on_tensor(xh_, y_, c_):
        return (dp, (xh_ * 4 + y_ % 4) * 2 + c_)

    x_peer = ((1 - xl) * 4 + z, t)
    z_peer = [(xl * 4 + (z + r) % 4, t) for r in range(4)]
    sibling = on_tensor(xh, y, 1 - c)
    far_chip = on_tensor(1 - xh, y, c)
    y_chip = [on_tensor(xh, y + r, c) for r in range(4)]
    y_of = (0, 3, 1, 2)

    sends = []

    def send(src, dst, dev):
        i = len(sends)
        copy = pltpu.make_async_remote_copy(
            src_ref=src, dst_ref=dst, send_sem=ss.at[i], recv_sem=rs.at[i],
            device_id=dev, device_id_type=MESH,
        )
        copy.start()
        sends.append(copy)
        return copy

    def got(*copies):
        for copy in copies:
            copy.wait_recv()

    def r16(i, base=0):
        return pl.ds(pl.multiple_of(base + i * 16, 16), 16)

    def r64(i, base=0):
        return pl.ds(pl.multiple_of(base + i * LEN, LEN), LEN)

    loads = []
    for i, (src, dst) in enumerate(((wg_hbm, wg_ref), (wu_hbm, wu_ref), (wd_hbm, wd_ref))):
        load = pltpu.make_async_copy(src, dst, loc.at[i])
        load.start()
        loads.append(load)

    bar = pltpu.get_barrier_semaphore()
    peers = [x_peer, sibling, far_chip] + z_peer[1:] + y_chip[1:]
    for dev in peers:
        pl.semaphore_signal(bar, inc=1, device_id=dev, device_id_type=MESH)
    xg[0, 0:LEN, :] = x_ref[...]
    xg[1, 0:LEN, :] = g_ref[...]
    pl.semaphore_wait(bar, len(peers))

    def seqs(p, k, n=1):
        return xg.at[:, pl.ds(p * 256 + k * LEN, n * LEN), :]

    mine, theirs = seqs(0, 0), seqs(0, 1)
    i_far = send(mine, seqs(0, 1), far_chip)
    i_sib = send(mine, seqs(0, 2), sibling)
    i_y = {1: send(mine, seqs(1, 0), y_chip[1]), 2: send(mine, seqs(2, 0), y_chip[3])}
    i_y[3] = send(mine, seqs(3, 0), y_chip[2])
    got(i_far)
    i_sib2 = send(theirs, seqs(0, 3), sibling)
    i_y2 = {1: send(theirs, seqs(1, 1), y_chip[1]), 2: send(theirs, seqs(2, 1), y_chip[3])}
    i_y2[3] = send(theirs, seqs(3, 1), y_chip[2])
    i_s = {}
    def gather(p):
        if p == 0:
            got(i_sib, i_sib2)
        else:
            got(i_y[p], i_y2[p])
            i_s[p] = send(seqs(p, 0, 2), seqs(p, 2, 2), sibling)
            got(i_s[p])

    s_a, s_b, s_c, s_z, s_x = {}, {}, {}, {}, {}

    lane = lax.broadcasted_iota(jnp.int32, (1, 128), 1)

    def first_half(v):
        return jnp.where(lane < 64, v, 0.0)

    def acc(start, n=16):
        return pl.ds(pl.multiple_of(start, 16), n)

    def keep(p, start, n=16):
        return pl.ds(pl.multiple_of(256 + p * 128 + start, 16), n)

    def make_ends():
        for load in loads:
            load.wait()
        g_end, u_end, d_end = (
            jnp.concatenate([w[:, MAIN:].astype(F32), jnp.zeros((feat, 64), F32)], 1)
            for w in (wg_ref, wu_ref, wd_ref)
        )
        ends[0] = (g_end + pltpu.roll(u_end, 64, 1)).astype(BF)
        ends[1] = d_end.astype(BF)
        ends[2] = pltpu.roll(g_end, 64, 1).astype(BF)
        ends[3] = u_end.astype(BF)

    def products(p):
        gather(p)
        xs = xg[0, p * 256 : p * 256 + 256, :]
        gs = xg[1, p * 256 : p * 256 + 256, :]
        for at, left, right in (
            (0, xs, wg_ref[:, :MAIN]),
            (MAIN, xs, wu_ref[:, :MAIN]),
            (2 * MAIN, gs, wd_ref[:, :MAIN]),
            (3 * MAIN, xs, ends[0]),
            (3 * MAIN + 128, gs, ends[1]),
        ):
            pool[0:256, at : at + right.shape[1]] = jnp.dot(left, right, preferred_element_type=F32)
        st_a[p] = pool[acc((1 - xl) * 64, 64), :].astype(BF)
        s_a[p] = send(st_a.at[p], xa.at[p], x_peer)
        st_b[p, 0, 0:16, :] = pool[acc(128 + 16 * zf), :].astype(BF)
        st_b[p, 0, 16:32, :] = pool[acc(192 + 16 * zp), :].astype(BF)
        st_b[p, 1, 0:16, :] = pool[acc(192 + 16 * zf), :].astype(BF)
        st_b[p, 1, 16:32, :] = pool[acc(128 + 16 * zm), :].astype(BF)
        s_b[p] = (
            send(st_b.at[p, 0], zb.at[p, 0], z_peer[1]),
            send(st_b.at[p, 1], zb.at[p, 1], z_peer[3]),
        )
        pool[keep(p, 0, 64), :] = pool[acc(xl * 64, 64), :]
        pool[keep(p, 64), :] = pool[acc(128 + 16 * zp), :]
        pool[keep(p, 80), :] = pool[acc(192 + 16 * zm), :]
        pool[keep(p, 96), :] = pool[acc(128 + 16 * z), :]
        pool[keep(p, 112), :] = pool[acc(192 + 16 * z), :]

    def second(p):
        sent = []
        for d, peer in ((0, z_peer[1]), (1, z_peer[3])):
            got(s_b[p][d])
            st_c[p, d] = (
                pool[keep(p, 64 + 16 * d), :] + zb[p, d, 0:16, :].astype(F32)
            ).astype(BF)
            sent.append(send(st_c.at[p, d], zc.at[p, d], peer))
        s_c[p] = sent
        got(s_a[p])
        sent = []
        for r in (2, 1, 3):
            zz = (z + r) % 4
            st_z[p, r - 1] = (
                pool[keep(p, 16 * zz), :] + xa[p, r16(zz), :].astype(F32)
            ).astype(BF)
            sent.append(send(st_z.at[p, r - 1], za.at[p, r - 1], z_peer[r]))
        s_z[p] = sent

    def third(p):
        got(*s_c[p])
        v0 = pool[keep(p, 96), :] + zc[p, 0].astype(F32) + zb[p, 1, 16:32, :].astype(F32)
        v1 = pool[keep(p, 112), :] + zc[p, 1].astype(F32) + zb[p, 0, 16:32, :].astype(F32)
        st_x[p] = jnp.where(xl == 0, v1, v0).astype(BF)
        pool[keep(p, 64), :] = jnp.where(xl == 0, v0, v1)
        s_x[p] = send(st_x.at[p], xb.at[p], x_peer)

    def activate(p, k, total):
        seq = ((xh + xl) % 2 * 4 + (y + y_of[p]) % 4) * 2 + (c + k // 2) % 2
        level = gran_ref[seq]
        width = jnp.where(
            level == 0, 2688, jnp.where(level == 1, 5376, jnp.where(level == 2, 10752, 21504))
        )

        def pointwise(gate_pre, up_pre, hidden_grad, first_col):
            n = gate_pre.shape[1]
            col = t * cols + first_col + lax.broadcasted_iota(jnp.int32, (1, n), 1)
            mask = jnp.where(col < width, 1.0, 0.0).astype(F32)
            sig = jax.nn.sigmoid(gate_pre)
            act = gate_pre * sig
            gate_delta = hidden_grad * up_pre * sig * (1.0 + gate_pre * (1.0 - sig)) * mask
            return act * up_pre * mask, gate_delta, hidden_grad * act * mask

        at = 4 * p + k + xl
        main = pointwise(total(0, MAIN), total(MAIN, MAIN), total(2 * MAIN, MAIN), 0)
        for i, v in enumerate(main):
            hid[at, r16(z), i * MAIN : (i + 1) * MAIN] = v.astype(BF)
        both = total(3 * MAIN, 128)
        gate_end, up_end = first_half(both), first_half(pltpu.roll(both, 64, 1))
        h, gd, ud = pointwise(gate_end, up_end, total(3 * MAIN + 128, 128), MAIN)
        end = first_half(h) + pltpu.roll(first_half(gd), 64, 1)
        hid[at, r16(z), 3 * MAIN : 3 * MAIN + 128] = end.astype(BF)
        hid[at, r16(z), 3 * MAIN + 128 :] = first_half(ud).astype(BF)

    h_az, h_ax, h_bx, h_bz, h_bf = {}, {}, {}, {}, {}

    def share(src, dev):
        return send(src, src, dev)

    def owned(p):
        got(*s_z[p])

        def total_a(at, n):
            v = pool[keep(p, 16 * z), at : at + n] + xa[p, r16(z), at : at + n].astype(F32)
            for r in range(3):
                v = v + za[p, r, :, at : at + n].astype(F32)
            return v

        def total_b(at, n):
            return pool[keep(p, 64), at : at + n] + xb[p, :, at : at + n].astype(F32)

        activate(p, 0, total_a)
        part = hid.at[4 * p + xl, r16(z), :]
        h_az[p] = {r: share(part, z_peer[r]) for r in (2, 1, 3)}
        h_ax[p] = [share(part, x_peer)]
        got(s_x[p])
        activate(p, 2, total_b)
        h_bx[p] = share(hid.at[4 * p + 2 + xl, r16(z), :], x_peer)

    def spread(p):
        got(h_bx[p])
        part = hid.at[pl.ds(4 * p + 2, 2), r16(z), :]
        h_bz[p] = (share(part, z_peer[1]), share(part, z_peer[3]))
        for r in (1, 3, 2):
            got(h_az[p][r])
            h_ax[p].append(share(hid.at[4 * p + xl, r16((z + 4 - r) % 4), :], x_peer))

    def forward(p):
        got(h_bz[p][0])
        one = share(hid.at[4 * p + 2, r16(zm), :], z_peer[1])
        got(h_bz[p][1])
        two = share(hid.at[4 * p + 3, r16(zp), :], z_peer[3])
        h_bf[p] = (one, two)

    s_o, s_y = {}, {}

    def output_rows(p, first, n):
        seq = 4 * p + first // LEN

        def part(at, size=MAIN):
            return hid[seq : seq + n // LEN, :, at : at + size].reshape(n, size)

        o = contract(part(0), wd_ref[:, :MAIN], 1, 1) + contract(part(3 * MAIN, 128), ends[1], 1, 1)
        d = contract(part(MAIN), wg_ref[:, :MAIN], 1, 1)
        d = d + contract(part(2 * MAIN), wu_ref[:, :MAIN], 1, 1)
        d = d + contract(part(3 * MAIN, 128), ends[2], 1, 1)
        return o, d + contract(part(3 * MAIN + 128, 128), ends[3], 1, 1)

    def outputs(p):
        got(*h_ax[p], *h_bf[p])
        for i, v in enumerate(output_rows(p, 0, 256)):
            sib_st[p, i] = v[128:, :]
            o_own[p % 2, i] = v[:128, :]
        s_o[p] = send(sib_st.at[p], sib_rx.at[p], sibling)

    def outputs_in_halves(p):
        got(*h_bf[p])
        for i, v in enumerate(output_rows(p, 128, 128)):
            sib_st[p, i] = v
        s_o[p] = send(sib_st.at[p], sib_rx.at[p], sibling)
        got(*h_ax[p])
        for i, v in enumerate(output_rows(p, 0, 128)):
            o_own[p % 2, i] = v

    grads = (
        ((1, 0, MAIN, pool), (1, 3 * MAIN, 128, pool_end)),
        ((0, MAIN, MAIN, pool),),
        ((0, 2 * MAIN, MAIN, pool), (0, 3 * MAIN, 256, pool)),
    )
    stores = []

    def weight_grads(n, p, rounds, last=False):
        for side, at, size, total in grads[n]:
            right = hid[4 * p : 4 * (p + rounds), :, at : at + size].reshape(256 * rounds, size)
            where = 0 if total is pool_end else at
            for i in range(0, feat, 256):
                rows = slice(i, min(i + 256, feat))
                left = xg[side, 256 * p : 256 * (p + rounds), rows]
                v = contract(left, right, 0, 0)
                if rounds == 1:
                    v = total[rows, where : where + size] + v
                if last and size == MAIN:
                    stage[n, rows, 0:MAIN] = v.astype(BF)
                else:
                    total[rows, where : where + size] = v

    def finish_grads(n, dst):
        weight_grads(n, 0, 1, True)
        if n == 0:
            end = pool_end[...]
        elif n == 1:
            end = pltpu.roll(pool[0:feat, 3 * MAIN : 3 * MAIN + 128], 64, 1)
        else:
            end = pool[0:feat, 3 * MAIN + 128 :]
        stage[n, :, MAIN:] = end[:, 0:64].astype(BF)
        copy = pltpu.make_async_copy(stage.at[n], dst, loc.at[3 + n])
        copy.start()
        stores.append(copy)

    def between_cores(p):
        got(s_o[p])
        if p == 0:
            o_own[0] = o_own[0] + sib_rx[0]
        else:
            st_y[p - 1] = (o_own[p % 2] + sib_rx[p]).astype(BF)
            s_y[p] = send(st_y.at[p - 1], y_rx.at[p - 1], y_chip[y_of[p]])

    make_ends()
    products(0)
    products(1)
    second(0)
    products(2)
    second(1)
    third(0)
    third(1)
    owned(1)
    second(2)
    spread(1)
    products(3)
    third(2)
    forward(1)
    owned(2)
    second(3)
    spread(2)
    outputs(1)
    third(3)
    forward(2)
    between_cores(1)
    owned(3)
    outputs(2)
    spread(3)
    owned(0)
    between_cores(2)
    weight_grads(0, 1, 2)
    forward(3)
    spread(0)
    weight_grads(1, 1, 2)
    outputs(3)
    weight_grads(2, 1, 2)
    between_cores(3)
    forward(0)
    weight_grads(0, 3, 1)
    weight_grads(1, 3, 1)
    weight_grads(2, 3, 1)
    outputs_in_halves(0)
    between_cores(0)

    got(s_y[1], s_y[2], s_y[3])
    for i in range(2):
        v = o_own[0, i]
        for p in range(3):
            v = v + y_rx[p, i].astype(F32)
        o_own[0, i] = v
        st_w[i] = v[LEN:, :].astype(BF)
    last = send(st_w, w_rx, far_chip)
    for n, dst in ((0, down_out), (2, up_out), (1, gate_out)):
        finish_grads(n, dst)
    got(last)
    out_ref[...] = (o_own[0, 0, 0:LEN, :] + w_rx[0].astype(F32)).astype(BF)
    dx_ref[...] = (o_own[0, 1, 0:LEN, :] + w_rx[1].astype(F32)).astype(BF)

    for copy in sends:
        copy.wait_send()
    for copy in stores:
        copy.wait()
    assert len(sends) == N_SENDS


MAIN = 1280
WIDE = 4096
N_SENDS = 12 + 4 * 22 + 3 + 1


def move(*refs):
    loads, stores = refs[-2], refs[-1]
    n = loads.shape[0]
    reads = [
        pltpu.make_async_copy(refs[i], refs[2 * n + i], loads.at[i]) for i in range(n)
    ]
    writes = [
        pltpu.make_async_copy(refs[2 * n + i], refs[n + i], stores.at[i]) for i in range(n)
    ]
    for copy in reads:
        copy.start()
    for read, write in zip(reads, writes):
        read.wait()
        write.start()
    for copy in writes:
        copy.wait()


def local(layer_input, gate_weight, up_weight, down_weight, granularity, out_grad):
    feat, cols = gate_weight.shape
    vm = pl.BlockSpec(memory_space=pltpu.VMEM)
    hbm = pl.BlockSpec(memory_space=pl.ANY)
    sm = pl.BlockSpec(memory_space=pltpu.SMEM)
    side = jax.ShapeDtypeStruct((LEN, feat), BF)
    weight = jax.ShapeDtypeStruct((feat, cols), BF)
    results = (side, side, weight, weight, weight)
    parts = pl.pallas_call(
        kernel,
        out_shape=results,
        in_specs=[sm, vm, vm, hbm, hbm, hbm],
        out_specs=(vm, vm, hbm, hbm, hbm),
        scratch_shapes=[
            pltpu.VMEM((feat, cols), BF),
            pltpu.VMEM((feat, cols), BF),
            pltpu.VMEM((feat, cols), BF),
            pltpu.VMEM((4, feat, 128), BF),
            pltpu.VMEM((2, 1024, feat), BF),
            pltpu.VMEM((16, LEN, WIDE), BF),
            pltpu.VMEM((256 + 4 * 128, WIDE), F32),
            pltpu.VMEM((feat, 128), F32),
            pltpu.VMEM((3, feat, cols), BF),
            pltpu.VMEM((4, LEN, WIDE), BF),
            pltpu.VMEM((4, LEN, WIDE), BF),
            pltpu.VMEM((4, 2, 32, WIDE), BF),
            pltpu.VMEM((4, 2, 32, WIDE), BF),
            pltpu.VMEM((4, 2, 16, WIDE), BF),
            pltpu.VMEM((4, 2, 16, WIDE), BF),
            pltpu.VMEM((4, 3, 16, WIDE), BF),
            pltpu.VMEM((4, 3, 16, WIDE), BF),
            pltpu.VMEM((4, 16, WIDE), BF),
            pltpu.VMEM((4, 16, WIDE), BF),
            pltpu.VMEM((2, 2, 128, feat), F32),
            pltpu.VMEM((4, 2, 128, feat), F32),
            pltpu.VMEM((4, 2, 128, feat), F32),
            pltpu.VMEM((3, 2, 128, feat), BF),
            pltpu.VMEM((3, 2, 128, feat), BF),
            pltpu.VMEM((2, LEN, feat), BF),
            pltpu.VMEM((2, LEN, feat), BF),
            pltpu.SemaphoreType.DMA((N_SENDS,)),
            pltpu.SemaphoreType.DMA((N_SENDS,)),
            pltpu.SemaphoreType.DMA((6,)),
        ],
        compiler_params=pltpu.CompilerParams(
            collective_id=0, has_side_effects=True, vmem_limit_bytes=62 << 20
        ),
        cost_estimate=pl.CostEstimate(flops=17_000_000_000, bytes_accessed=20_000_000, transcendentals=0),
    )(granularity, layer_input, out_grad, gate_weight, up_weight, down_weight.T)
    out, dx, gate_grad, up_grad, down_grad = pl.pallas_call(
        move,
        out_shape=results,
        in_specs=[hbm] * 5,
        out_specs=(hbm,) * 5,
        scratch_shapes=[pltpu.VMEM(r.shape, BF) for r in results]
        + [pltpu.SemaphoreType.DMA((5,))] * 2,
        compiler_params=pltpu.CompilerParams(vmem_limit_bytes=62 << 20),
        cost_estimate=pl.CostEstimate(flops=0, bytes_accessed=11_000_000, transcendentals=0),
    )(*parts)
    return out, dx, gate_grad, up_grad, down_grad.T


def solution(mesh):
    in_specs = (
        P("tensor", "dp"),
        P("dp", "tensor"),
        P("dp", "tensor"),
        P("tensor", "dp"),
        P(),
        P("tensor", "dp"),
    )
    out_specs = (
        P("tensor", "dp"),
        P("tensor", "dp"),
        P("dp", "tensor"),
        P("dp", "tensor"),
        P("tensor", "dp"),
    )
    return jax.shard_map(local, mesh=mesh, in_specs=in_specs, out_specs=out_specs, check_vma=False)
```
